32 devices in a mesh: dp: 16 (over z, y, x), group: 2 (over core).
Axes of the slice: x: 2, y: 2, z: 4, core: 2. Of those that a mesh axis runs over, the one named last changes fastest.
Arguments:
- queries: bfloat16 [12288, 4096], P('dp', 'group'), may hold values from -120 to 120
- passages: bfloat16 [12288, 4096], P('dp', 'group'), may hold values from -120 to 120
- neg_owner: int32 [12288, 8], P('dp'), may hold values from 0 to 15, all different within a row; in each aligned block of 768 rows (0 to 767, 768 to 1535, ...) at most 480 rows name the same one
- neg_row: int32 [12288, 8], P('dp'), may hold values from 0 to 767
- gain: float32 [4096], replicated, may hold values from 0.5 to 1.5
Outputs:
- grad_queries: bfloat16 [12288, 4096], P('dp', 'group')
- grad_passages: bfloat16 [12288, 4096], P('dp', 'group')
- grad_gain: float32 [4096], replicated
- loss: float32 [], replicated
The draws below stay inside these ranges and needn't reach their ends.
Inputs may be any that keep to these rules, and one draw needn't show every extreme that they name: `neg_owner`: the 8 owners of one query are distinct; among the 768 queries of one data group no owner is named more than 480 times, and that many in every draw.
All inputs are finite; a program needn't handle non-finite values.
Results may differ from the reference program's by a relative error of at most 0.00305.
The reference program's roundings to bfloat16 on the way count: a program that leaves them out, or rounds other values in their place, can miss the bound.
Values may be sent and summed in bfloat16 or wider, within the bound.
A program may use at most 192 MiB of HBM per device.

```python
import math
import jax
import jax.numpy as jnp
import numpy as np
from jax import lax

VECTOR_LENGTH = 4096
BATCH = 768
NEG = 8
CAP = 480
QUERIES = 12288
N_DP = 16


def common_direction(key):
    return jax.random.uniform(jax.random.fold_in(key, 31), (1, VECTOR_LENGTH), jnp.float32, -1.7, 1.7)


def passage_rows(key, direction, fraction):
    normal_part = jnp.clip(jax.random.normal(jax.random.fold_in(key, 21), (QUERIES, VECTOR_LENGTH), jnp.float32), -4.0, 4.0)
    rough = normal_part
    rough = jnp.sqrt(fraction) * direction + jnp.sqrt(1.0 - fraction) * rough
    row_scale = jnp.exp(jax.random.uniform(jax.random.fold_in(key, 23), (QUERIES, 1), jnp.float32, 0.0, math.log(10.0)))
    col_scale = jnp.exp(jax.random.uniform(jax.random.fold_in(key, 24), (1, VECTOR_LENGTH), jnp.float32, 0.0, math.log(3.0)))
    values = rough * row_scale * col_scale
    placed = (jnp.arange(QUERIES) % BATCH == 8)[:, None]
    return jnp.where(placed, values, values)


def draw_passages(key, part):
    passage_share = 0.0
    direction = common_direction(key)
    return passage_rows(key, direction, passage_share).astype(jnp.bfloat16)


def draw_queries(key, part):
    query_share = 0.0
    direction = common_direction(key)
    key = jax.random.fold_in(key, 3)
    fraction = query_share * jax.random.uniform(jax.random.fold_in(key, 41), (QUERIES, 1), jnp.float32)
    private = passage_rows(key, direction, fraction)
    placed = (jnp.arange(QUERIES) % BATCH == 3)[:, None]
    aligned = private
    return jnp.where(placed, aligned, private).astype(jnp.bfloat16)


def plant(values, key, low, top_value):
    longest = values.shape.index(max(values.shape))
    spots = []
    for shift in (0, 1):
        where = [jax.random.randint(jax.random.fold_in(key, axis), (), 0, length) for axis, length in enumerate(values.shape)]
        where[longest] = (where[longest] + shift) % values.shape[longest]
        spots.append(tuple(where))
    return values.at[spots[0]].set(low).at[spots[1]].set(top_value)


def rank_table(count, skew):
    weights = [(1 << 20) // math.isqrt(grade ** skew) + 1 for grade in range(1, count + 1)]
    scale = 1 + sum(weights) // (1 << 30)
    return np.cumsum(np.array([max(1, weight // scale) for weight in weights]))


def skewed_ids(key, extent, count, lean):
    table = rank_table(count, lean)
    lot = jax.random.randint(jax.random.fold_in(key, 1), extent, 0, int(table[count - 1]))
    grade = jnp.searchsorted(jnp.asarray(table, jnp.int32), lot, side="right")
    return jax.random.permutation(jax.random.fold_in(key, 2), count)[grade].astype(jnp.int32)


def assign_block(key, own, number, rows, amount, top, bound, skew):
    sequence = jax.random.permutation(key, amount)
    crowded, ordinary = shares(amount, rows * top, bound, skew, True), shares(amount, rows * top, bound, skew, False)
    places = jnp.arange(amount)

    def named(tallies, rotation):
        used = int((tallies > 0).sum())
        fixed = max(1, used // 4)
        passed = fixed + (places - fixed + rotation * (used - fixed)) % max(1, amount - fixed)
        return jnp.zeros((amount,), jnp.int32).at[sequence[jnp.where(places < fixed, places, passed)]].set(jnp.asarray(tallies, jnp.int32))

    tallies = jnp.where(number % 4 == 0, named(crowded, number // 4), named(ordinary, number - number // 4 - 1))
    mixed = jax.random.permutation(jax.random.fold_in(own, 3), amount)
    giver, receiver = mixed[0:amount // 2 * 2:2], mixed[1:amount // 2 * 2:2]
    margin = jnp.minimum(tallies[giver] - 1, bound - tallies[receiver]) // 2
    margin = jnp.where((giver == sequence[0]) | (receiver == sequence[0]) | (tallies[receiver] == 0), 0, jnp.maximum(margin, 0))
    passed = jax.random.randint(jax.random.fold_in(own, 4), (amount // 2,), 0, 1 << 20) % (margin + 1)
    tallies = tallies.at[giver].add(-passed).at[receiver].add(passed)
    items = jnp.searchsorted(jnp.cumsum(tallies), jnp.arange(rows * top), side="right").astype(jnp.int32)
    table = items.reshape(top, rows).T
    table = table[jax.random.permutation(jax.random.fold_in(own, 1), rows)]
    rotation = jax.random.randint(jax.random.fold_in(own, 2), (rows, 1), 0, top)
    return jnp.take_along_axis(table, (jnp.arange(top)[None, :] + rotation) % top, axis=1)


def shares(amount, total, limit, lean, full):
    portions = [(1 << 20) // math.isqrt(standing ** lean) + 1 for standing in range(1, amount + 1)]
    largest = limit if full else min(limit, max(-(-total // amount), total * portions[0] // sum(portions)))
    least = 1 if total - largest >= amount - 1 else 0
    holding, rest = [largest] + [least] * (amount - 1), total - largest - least * (amount - 1)
    while rest > 0:
        free = [i for i in range(1, amount) if holding[i] < largest] or [i for i in range(1, amount) if holding[i] < limit]
        pool, remaining = sum([portions[i] for i in free]), rest
        for i in free:
            more = min(limit - holding[i], max(1, remaining * portions[i] // pool), rest)
            holding[i] = holding[i] + more
            rest = rest - more
    return np.array(holding)


def setup_inputs(seed: int = 0) -> dict:
    streams_of = jax.random.split(jax.random.key(seed), 6)
    queries = draw_queries(jax.random.fold_in(streams_of[5], 71), 0)
    passages = draw_passages(jax.random.fold_in(streams_of[5], 71), 0)
    neg_owner_keys = jax.random.split(jax.random.fold_in(streams_of[2], 1), QUERIES // BATCH)
    neg_owner_turns = jax.random.permutation(jax.random.fold_in(streams_of[2], 3), QUERIES // BATCH)
    neg_owner = jax.vmap(lambda own, number: assign_block(jax.random.fold_in(streams_of[2], 2), own, number, BATCH, N_DP, NEG, CAP, 2))(neg_owner_keys, neg_owner_turns).reshape((QUERIES, NEG))
    neg_row = plant(skewed_ids(streams_of[3], (QUERIES, NEG), BATCH, 2), jax.random.fold_in(streams_of[3], 3), 0, BATCH - 1).astype(jnp.int32)
    gain = jnp.clip(1.0 + 0.1 * jax.random.normal(streams_of[4], (VECTOR_LENGTH,), jnp.float32), 0.5, 1.5)
    return {"queries": queries, "passages": passages, "neg_owner": neg_owner, "neg_row": neg_row, "gain": gain}


EPSILON = 1e-06
SOFTNESS_DIVISOR = 0.25

def embed(rows, gain):
    values = rows.astype(jnp.float32)
    inverse = lax.rsqrt(lax.optimization_barrier(jnp.mean(values * values, axis=1, keepdims=True)) + EPSILON)
    normed = values * inverse
    return ((normed * gain).astype(jnp.bfloat16), normed, inverse)

def norm_back(grad_emb, normed, inverse, gain):
    inner = grad_emb * gain
    return inverse * (inner - normed * lax.optimization_barrier(jnp.mean(inner * normed, axis=1, keepdims=True)))

def reference(queries, passages, neg_owner, neg_row, gain):
    multiplier_coefficient = 1.0 / (SOFTNESS_DIVISOR * math.sqrt(VECTOR_LENGTH))
    q_emb, q_normed, q_inverse = embed(queries, gain)
    p_emb, p_normed, document_reciprocal_norm = embed(passages, gain)
    neg_ids = (neg_owner * BATCH + neg_row).astype(jnp.int32)

    def block(carry, index):
        start = (index * BATCH).astype(jnp.int32)
        q_blk = lax.dynamic_slice_in_dim(q_emb, start, BATCH, 0)
        p_blk = lax.dynamic_slice_in_dim(p_emb, start, BATCH, 0)
        id_blk = lax.dynamic_slice_in_dim(neg_ids, start, BATCH, 0)
        hard = jnp.take(p_emb, id_blk.reshape(-1), axis=0).reshape(BATCH, NEG, VECTOR_LENGTH)
        scores = jnp.dot(q_blk, p_blk.T, preferred_element_type=jnp.float32) * multiplier_coefficient
        near = jnp.einsum('qd,qkd->qk', q_blk.astype(jnp.float32), hard.astype(jnp.float32)) * multiplier_coefficient
        top = jnp.maximum(lax.optimization_barrier(jnp.max(scores, axis=1)), lax.optimization_barrier(jnp.max(near, axis=1)))[:, None]
        total = lax.optimization_barrier(jnp.sum(jnp.exp(scores - top), axis=1, keepdims=True)) + lax.optimization_barrier(jnp.sum(jnp.exp(near - top), axis=1, keepdims=True))
        lse = top + jnp.log(total)
        losses = lse[:, 0] - jnp.diagonal(scores)
        eye = jnp.eye(BATCH, dtype=jnp.float32)
        weights = (jnp.exp(scores - lse) - eye).astype(jnp.bfloat16)
        hard_weights = jnp.exp(near - lse).astype(jnp.bfloat16)
        grad_q = (jnp.dot(weights, p_blk, preferred_element_type=jnp.float32) + jnp.einsum('qk,qkd->qd', hard_weights.astype(jnp.float32), hard.astype(jnp.float32))) * multiplier_coefficient
        grad_p = jnp.dot(weights.T, q_blk, preferred_element_type=jnp.float32) * multiplier_coefficient
        pair = ((hard_weights.astype(jnp.float32) * multiplier_coefficient)[:, :, None] * q_blk.astype(jnp.float32)[:, None, :]).astype(jnp.bfloat16)
        carry = carry.at[id_blk.reshape(-1)].add(pair.reshape(-1, VECTOR_LENGTH).astype(jnp.float32))
        return (carry, (grad_q, grad_p, losses))
    hard_total, (grad_q, grad_p, losses) = lax.scan(block, jnp.zeros((QUERIES, VECTOR_LENGTH), jnp.float32), jnp.arange(N_DP, dtype=jnp.int32))
    grad_q = grad_q.reshape(QUERIES, VECTOR_LENGTH)
    grad_p = grad_p.reshape(QUERIES, VECTOR_LENGTH) + hard_total
    grad_queries = norm_back(grad_q, q_normed, q_inverse, gain).astype(jnp.bfloat16)
    grad_passages = norm_back(grad_p, p_normed, document_reciprocal_norm, gain).astype(jnp.bfloat16)
    grad_gain = (lax.optimization_barrier(jnp.sum(grad_q * q_normed, axis=0)) + lax.optimization_barrier(jnp.sum(grad_p * p_normed, axis=0))) / math.sqrt(QUERIES)
    loss = jnp.sum(losses) / QUERIES
    return (grad_queries, grad_passages, grad_gain, loss)
```

```python
import functools
import math

import jax
import jax.numpy as jnp
from jax import lax
from jax.experimental import pallas as pl
from jax.experimental.pallas import tpu as pltpu
from jax.sharding import PartitionSpec as P

EPSILON = 1e-06
SOFTNESS_DIVISOR = 0.25
ROWS_BY_ROWS = (((1,), (1,)), ((), ()))
COLS_BY_COLS = (((0,), (0,)), ((), ()))
VMEM_BYTES = 56 << 20


def column(table, index):
    lane = lax.broadcasted_iota(jnp.int32, table.shape, 1)
    return jnp.sum(jnp.where(lane == index, table, jnp.zeros_like(table)), axis=1, keepdims=True)


def near_kernel(q_ref, p_ref, wanted_ref, near_ref):
    step = pl.program_id(0)

    @pl.when(step == 0)
    def _():
        near_ref[...] = jnp.zeros_like(near_ref)

    products = lax.dot_general(
        q_ref[...], p_ref[0], ROWS_BY_ROWS, preferred_element_type=jnp.float32
    )
    wanted = column(wanted_ref[...], step)
    place = lax.broadcasted_iota(jnp.int32, products.shape, 1)
    picked = jnp.sum(jnp.where(place == wanted, products, 0.0), axis=1, keepdims=True)
    lane = lax.broadcasted_iota(jnp.int32, near_ref.shape, 1)
    near_ref[...] += jnp.where(lane == step, picked, 0.0)


def grad_q_kernel(weights_ref, own_ref, p_ref, wanted_ref, hard_ref, grad_ref):
    step = pl.program_id(0)

    @pl.when(step == 0)
    def _():
        grad_ref[...] = jnp.dot(
            weights_ref[...], own_ref[...], preferred_element_type=jnp.float32
        )

    wanted = column(wanted_ref[...], step)
    hard = column(hard_ref[...], step)
    place = lax.broadcasted_iota(jnp.int32, weights_ref.shape, 1)
    spread = jnp.where(place == wanted, hard, 0.0).astype(jnp.bfloat16)
    grad_ref[...] += jnp.dot(spread, p_ref[0], preferred_element_type=jnp.float32)


def grad_p_kernel(scale, weights_ref, own_ref, q_ref, asked_ref, hard_ref, grad_ref):
    step = pl.program_id(0)

    @pl.when(step == 0)
    def _():
        grad_ref[...] = scale * lax.dot_general(
            weights_ref[...], own_ref[...], COLS_BY_COLS, preferred_element_type=jnp.float32
        )

    hard = column(hard_ref[...], step) * scale
    pairs = (hard * q_ref[0].astype(jnp.float32)).astype(jnp.bfloat16)
    row = lax.broadcasted_iota(jnp.int32, weights_ref.shape, 0)
    select = jnp.where(row == asked_ref[0], 1.0, 0.0).astype(jnp.bfloat16)
    grad_ref[...] += jnp.dot(select, pairs, preferred_element_type=jnp.float32)


def whole(shape):
    return pl.BlockSpec(shape, lambda step: (0,) * len(shape))


def block(shape):
    return pl.BlockSpec((1,) + shape, lambda step: (step, 0, 0))


def call(kernel, blocks, in_specs, out_shape, rows, piece):
    return pl.pallas_call(
        kernel,
        grid=(blocks,),
        in_specs=in_specs,
        out_specs=whole(out_shape),
        out_shape=jax.ShapeDtypeStruct(out_shape, jnp.float32),
        compiler_params=pltpu.CompilerParams(vmem_limit_bytes=VMEM_BYTES),
        cost_estimate=pl.CostEstimate(
            flops=2 * blocks * rows * rows * piece,
            bytes_accessed=2 * blocks * rows * piece,
            transcendentals=0,
        ),
    )


def local(queries, passages, neg_owner, neg_row, gain):
    rows, piece = queries.shape
    n_data = lax.axis_size("dp")
    n_members = lax.axis_size("group")
    member = lax.axis_index("group")
    hidden = piece * n_members
    scale = 1.0 / (SOFTNESS_DIVISOR * math.sqrt(hidden))
    my_gain = lax.dynamic_slice_in_dim(gain, member * piece, piece, 0)
    q_values = queries.astype(jnp.float32)
    p_values = passages.astype(jnp.float32)
    q_square, p_square = lax.psum(
        (jnp.sum(q_values * q_values, axis=1), jnp.sum(p_values * p_values, axis=1)), "group"
    )
    q_inverse = lax.rsqrt(q_square / hidden + EPSILON)[:, None]
    p_inverse = lax.rsqrt(p_square / hidden + EPSILON)[:, None]
    q_emb = (q_values * q_inverse * my_gain).astype(jnp.bfloat16)
    p_emb = (p_values * p_inverse * my_gain).astype(jnp.bfloat16)

    all_p = lax.all_gather(p_emb, "dp", axis=0, tiled=False)
    q_later, _ = lax.optimization_barrier((q_emb, all_p))
    all_q = lax.all_gather(q_later, "dp", axis=0, tiled=False)

    owners = jnp.arange(n_data, dtype=jnp.int32)
    named = neg_owner[:, :, None] == owners[None, None, :]
    wanted = jnp.sum(jnp.where(named, neg_row[:, :, None] + 1, 0), axis=1) - 1

    partial_scores = jnp.dot(q_emb, p_emb.T, preferred_element_type=jnp.float32) * scale
    scores = lax.psum(partial_scores, "group")
    near_part = call(
        near_kernel,
        n_data,
        [whole((rows, piece)), block((rows, piece)), whole((rows, n_data))],
        (rows, n_data),
        rows,
        piece,
    )(q_emb, all_p, wanted)
    near = lax.psum(near_part * scale, "group")
    near = jnp.where(wanted >= 0, near, -jnp.inf)

    positive = (
        jnp.arange(rows, dtype=jnp.int32)[None, :] == jnp.arange(rows, dtype=jnp.int32)[:, None]
    )
    top = jnp.maximum(jnp.max(scores, axis=1), jnp.max(near, axis=1))[:, None]
    total = jnp.sum(jnp.exp(scores - top), axis=1, keepdims=True) + jnp.sum(
        jnp.exp(near - top), axis=1, keepdims=True
    )
    lse = top + jnp.log(total)
    losses = lse[:, 0] - jnp.sum(jnp.where(positive, scores, 0.0), axis=1)
    weights = (jnp.exp(scores - lse) - positive.astype(jnp.float32)).astype(jnp.bfloat16)
    hard = jnp.exp(near - lse).astype(jnp.bfloat16).astype(jnp.float32)

    share = rows // n_members
    loss_part = jnp.sum(lax.dynamic_slice_in_dim(losses, member * share, share, 0))

    sent = jnp.concatenate([wanted.T.astype(jnp.float32), hard.T], axis=1)
    came = lax.all_to_all(sent, "dp", split_axis=0, concat_axis=0, tiled=True)
    asked = came[:, :rows].astype(jnp.int32)[:, None, :]
    asked_hard = came[:, rows:].T

    grad_q = (
        call(
            grad_q_kernel,
            n_data,
            [
                whole((rows, rows)),
                whole((rows, piece)),
                block((rows, piece)),
                whole((rows, n_data)),
                whole((rows, n_data)),
            ],
            (rows, piece),
            rows,
            piece,
        )(weights, p_emb, all_p, wanted, hard)
        * scale
    )
    grad_p = call(
        functools.partial(grad_p_kernel, scale),
        n_data,
        [
            whole((rows, rows)),
            whole((rows, piece)),
            block((rows, piece)),
            block((1, rows)),
            whole((rows, n_data)),
        ],
        (rows, piece),
        rows,
        piece,
    )(weights, q_emb, all_q, asked, asked_hard)

    q_normed = q_values * q_inverse
    p_normed = p_values * p_inverse
    q_inner = grad_q * my_gain
    p_inner = grad_p * my_gain
    q_mean, p_mean = lax.psum(
        (jnp.sum(q_inner * q_normed, axis=1), jnp.sum(p_inner * p_normed, axis=1)), "group"
    )
    grad_queries = (q_inverse * (q_inner - q_normed * (q_mean / hidden)[:, None])).astype(
        jnp.bfloat16
    )
    grad_passages = (p_inverse * (p_inner - p_normed * (p_mean / hidden)[:, None])).astype(
        jnp.bfloat16
    )
    gain_part = jnp.sum(grad_q * q_normed, axis=0) + jnp.sum(grad_p * p_normed, axis=0)
    gain_full = lax.dynamic_update_slice_in_dim(
        jnp.zeros((hidden,), jnp.float32), gain_part, member * piece, 0
    )
    loss_total, gain_total = lax.psum((loss_part, gain_full), ("dp", "group"))
    count = rows * n_data
    return (grad_queries, grad_passages, gain_total / math.sqrt(count), loss_total / count)


def solution(mesh):
    return jax.shard_map(
        local,
        mesh=mesh,
        in_specs=(P("dp", "group"), P("dp", "group"), P("dp", None), P("dp", None), P()),
        out_specs=(P("dp", "group"), P("dp", "group"), P(), P()),
        check_vma=False,
    )
```

```python
import functools
import math

import jax
import jax.numpy as jnp
from jax import lax
from jax.experimental import pallas as pl
from jax.experimental.pallas import tpu as pltpu
from jax.sharding import PartitionSpec as P

EPSILON = 1e-06
SOFTNESS_DIVISOR = 0.25
ROWS_BY_ROWS = (((1,), (1,)), ((), ()))
COLS_BY_COLS = (((0,), (0,)), ((), ()))
VMEM_BYTES = 56 << 20


def column(table, index):
    lane = lax.broadcasted_iota(jnp.int32, table.shape, 1)
    return jnp.sum(jnp.where(lane == index, table, jnp.zeros_like(table)), axis=1, keepdims=True)


def near_kernel(q_ref, p_ref, wanted_ref, near_ref):
    step = pl.program_id(1)

    @pl.when(step == 0)
    def _():
        near_ref[...] = jnp.zeros_like(near_ref)

    products = lax.dot_general(
        q_ref[0], p_ref[0], ROWS_BY_ROWS, preferred_element_type=jnp.float32
    )
    wanted = column(wanted_ref[0], step)
    place = lax.broadcasted_iota(jnp.int32, products.shape, 1)
    picked = jnp.sum(jnp.where(place == wanted, products, 0.0), axis=1, keepdims=True)
    lane = lax.broadcasted_iota(jnp.int32, near_ref.shape[1:], 1)
    near_ref[0] += jnp.where(lane == step, picked, 0.0)


def add_q_term(p_ref, wanted_ref, hard_ref, total_ref, step):
    wanted = column(wanted_ref[...], step)
    hard = column(hard_ref[...], step)
    rows = wanted.shape[0]
    place = lax.broadcasted_iota(jnp.int32, (rows, rows), 1)
    spread = jnp.where(place == wanted, hard, 0.0).astype(jnp.bfloat16)
    total_ref[...] += jnp.dot(spread, p_ref[0], preferred_element_type=jnp.float32)


def add_p_term(scale, q_ref, asked_ref, hard_ref, total_ref, step):
    hard = column(hard_ref[...], step) * scale
    pairs = (hard * q_ref[0].astype(jnp.float32)).astype(jnp.bfloat16)
    rows = pairs.shape[0]
    row = lax.broadcasted_iota(jnp.int32, (rows, rows), 0)
    select = jnp.where(row == asked_ref[0], 1.0, 0.0).astype(jnp.bfloat16)
    total_ref[...] += jnp.dot(select, pairs, preferred_element_type=jnp.float32)


def own_q_kernel(weights_ref, own_ref, p_ref, wanted_ref, hard_ref, grad_ref):
    step = pl.program_id(0)

    @pl.when(step == 0)
    def _():
        grad_ref[...] = jnp.dot(
            weights_ref[...], own_ref[...], preferred_element_type=jnp.float32
        )

    add_q_term(p_ref, wanted_ref, hard_ref, grad_ref, step)


def own_p_kernel(scale, weights_ref, own_ref, q_ref, asked_ref, hard_ref, grad_ref):
    step = pl.program_id(0)

    @pl.when(step == 0)
    def _():
        grad_ref[...] = scale * lax.dot_general(
            weights_ref[...], own_ref[...], COLS_BY_COLS, preferred_element_type=jnp.float32
        )

    add_p_term(scale, q_ref, asked_ref, hard_ref, grad_ref, step)


def sent_q_kernel(p_ref, wanted_ref, hard_ref, grad_ref, total_ref):
    step = pl.program_id(0)

    @pl.when(step == 0)
    def _():
        total_ref[...] = jnp.zeros_like(total_ref)

    add_q_term(p_ref, wanted_ref, hard_ref, total_ref, step)

    @pl.when(step == pl.num_programs(0) - 1)
    def _():
        grad_ref[...] = total_ref[...].astype(grad_ref.dtype)


def sent_p_kernel(scale, q_ref, asked_ref, hard_ref, grad_ref, total_ref):
    step = pl.program_id(0)

    @pl.when(step == 0)
    def _():
        total_ref[...] = jnp.zeros_like(total_ref)

    add_p_term(scale, q_ref, asked_ref, hard_ref, total_ref, step)

    @pl.when(step == pl.num_programs(0) - 1)
    def _():
        grad_ref[...] = total_ref[...].astype(grad_ref.dtype)


def whole(shape):
    return pl.BlockSpec(shape, lambda step: (0,) * len(shape))


def block(shape):
    return pl.BlockSpec((1,) + shape, lambda step: (step, 0, 0))


def params():
    return pltpu.CompilerParams(vmem_limit_bytes=VMEM_BYTES)


def cost(blocks, rows, piece):
    return pl.CostEstimate(
        flops=2 * blocks * rows * rows * piece,
        bytes_accessed=2 * blocks * rows * piece,
        transcendentals=0,
    )


def call(kernel, blocks, in_specs, dtype, rows, piece):
    scratch = [] if dtype == jnp.float32 else [pltpu.VMEM((rows, piece), jnp.float32)]
    return pl.pallas_call(
        kernel,
        grid=(blocks,),
        in_specs=in_specs,
        out_specs=whole((rows, piece)),
        out_shape=jax.ShapeDtypeStruct((rows, piece), dtype),
        scratch_shapes=scratch,
        compiler_params=params(),
        cost_estimate=cost(blocks, rows, piece),
    )


def local(queries, passages, neg_owner, neg_row, gain):
    rows, piece = queries.shape
    n_data = lax.axis_size("dp")
    n_members = lax.axis_size("group")
    member = lax.axis_index("group")
    hidden = piece * n_members
    scale = 1.0 / (SOFTNESS_DIVISOR * math.sqrt(hidden))
    my_gain = lax.dynamic_slice_in_dim(gain, member * piece, piece, 0)
    q_values = queries.astype(jnp.float32)
    p_values = passages.astype(jnp.float32)
    q_square, p_square = lax.psum(
        (jnp.sum(q_values * q_values, axis=1), jnp.sum(p_values * p_values, axis=1)), "group"
    )
    q_inverse = lax.rsqrt(q_square / hidden + EPSILON)[:, None]
    p_inverse = lax.rsqrt(p_square / hidden + EPSILON)[:, None]
    q_emb = (q_values * q_inverse * my_gain).astype(jnp.bfloat16)
    p_emb = (p_values * p_inverse * my_gain).astype(jnp.bfloat16)

    lines = 2 ** (int(math.log2(n_data)) // 2)
    plane = n_data // lines
    line_groups = [[a * plane + b for a in range(lines)] for b in range(plane)]
    plane_groups = [[a * plane + b for b in range(plane)] for a in range(lines)]
    here = lax.rem(lax.axis_index("dp"), plane)

    def exchange(table, groups):
        flat = table.reshape(table.shape[0], -1)
        came = lax.all_to_all(
            flat, "dp", split_axis=0, concat_axis=0, axis_index_groups=groups, tiled=True
        )
        return came.reshape(table.shape)

    line_q = lax.all_gather(q_emb, "dp", axis_index_groups=line_groups)
    plane_p = lax.all_gather(p_emb, "dp", axis_index_groups=plane_groups)
    p_later, _ = lax.optimization_barrier((p_emb, line_q))
    line_p = lax.all_gather(p_later, "dp", axis_index_groups=line_groups)

    owners = jnp.arange(n_data, dtype=jnp.int32)[:, None, None]
    named = neg_owner.T[None] == owners
    wanted = (jnp.sum(jnp.where(named, neg_row.T[None] + 1, 0), axis=1) - 1).reshape(
        lines, plane, rows
    )
    line_wanted = exchange(wanted, line_groups)
    plane_wanted = exchange(wanted.transpose(1, 0, 2), plane_groups).transpose(0, 2, 1)

    partial_scores = jnp.dot(q_emb, p_emb.T, preferred_element_type=jnp.float32) * scale
    scores = lax.psum(partial_scores, "group")
    near_part = pl.pallas_call(
        near_kernel,
        grid=(lines, plane),
        in_specs=[
            pl.BlockSpec((1, rows, piece), lambda a, b: (a, 0, 0)),
            pl.BlockSpec((1, rows, piece), lambda a, b: (b, 0, 0)),
            pl.BlockSpec((1, rows, plane), lambda a, b: (a, 0, 0)),
        ],
        out_specs=pl.BlockSpec((1, rows, plane), lambda a, b: (a, 0, 0)),
        out_shape=jax.ShapeDtypeStruct((lines, rows, plane), jnp.float32),
        compiler_params=params(),
        cost_estimate=cost(n_data, rows, piece),
    )(line_q, plane_p, line_wanted.transpose(0, 2, 1))
    line_near = lax.psum(near_part.transpose(0, 2, 1) * scale, "group")
    near = jnp.where(wanted >= 0, exchange(line_near, line_groups), -jnp.inf)
    near = near.reshape(n_data, rows)

    positive = (
        jnp.arange(rows, dtype=jnp.int32)[None, :] == jnp.arange(rows, dtype=jnp.int32)[:, None]
    )
    top = jnp.maximum(jnp.max(scores, axis=1), jnp.max(near, axis=0))
    total = jnp.sum(jnp.exp(scores - top[:, None]), axis=1) + jnp.sum(
        jnp.exp(near - top[None, :]), axis=0
    )
    lse = top + jnp.log(total)
    losses = lse - jnp.sum(jnp.where(positive, scores, 0.0), axis=1)
    weights = (jnp.exp(scores - lse[:, None]) - positive.astype(jnp.float32)).astype(jnp.bfloat16)
    hard = jnp.exp(near - lse[None, :]).astype(jnp.bfloat16).astype(jnp.float32)
    hard = hard.reshape(lines, plane, rows)

    share = rows // n_members
    loss_part = jnp.sum(lax.dynamic_slice_in_dim(losses, member * share, share, 0))

    line_hard = exchange(hard, line_groups)
    plane_hard = exchange(hard.transpose(1, 0, 2), plane_groups).transpose(0, 2, 1)

    def partner_of(shift):
        return [
            (a * plane + b, a * plane + (b ^ shift)) for a in range(lines) for b in range(plane)
        ]

    def p_tables(target):
        asked = lax.dynamic_index_in_dim(line_wanted, target, 1, keepdims=True)
        asked_hard = lax.dynamic_index_in_dim(line_hard, target, 1, keepdims=False).T
        return asked, asked_hard

    def q_tables(target):
        return (
            lax.dynamic_index_in_dim(plane_wanted, target, 0, keepdims=False),
            lax.dynamic_index_in_dim(plane_hard, target, 0, keepdims=False),
        )

    p_specs = [block((rows, piece)), block((1, rows)), whole((rows, lines))]
    q_specs = [block((rows, piece)), whole((rows, lines)), whole((rows, lines))]
    batch_specs = [whole((rows, rows)), whole((rows, piece))]
    size = (rows, piece)
    shifts = range(plane - 1, 0, -1)

    p_parts = []
    for shift in shifts:
        part = call(
            functools.partial(sent_p_kernel, scale), lines, p_specs, jnp.bfloat16, *size
        )(line_q, *p_tables(here ^ shift))
        p_parts.append(lax.ppermute(part, "dp", partner_of(shift)))
    grad_p = call(
        functools.partial(own_p_kernel, scale), lines, batch_specs + p_specs, jnp.float32, *size
    )(weights, q_emb, line_q, *p_tables(here))
    q_parts = []
    for shift in shifts:
        part = call(sent_q_kernel, lines, q_specs, jnp.bfloat16, *size)(
            line_p, *q_tables(here ^ shift)
        )
        q_parts.append(lax.ppermute(part, "dp", partner_of(shift)))
    grad_q = call(own_q_kernel, lines, batch_specs + q_specs, jnp.float32, *size)(
        weights, p_emb, line_p, *q_tables(here)
    )
    for part in p_parts:
        grad_p = grad_p + part.astype(jnp.float32)
    for part in q_parts:
        grad_q = grad_q + part.astype(jnp.float32)
    grad_q = grad_q * scale

    q_normed = q_values * q_inverse
    p_normed = p_values * p_inverse
    q_inner = grad_q * my_gain
    p_inner = grad_p * my_gain
    q_mean, p_mean = lax.psum(
        (jnp.sum(q_inner * q_normed, axis=1), jnp.sum(p_inner * p_normed, axis=1)), "group"
    )
    grad_queries = (q_inverse * (q_inner - q_normed * (q_mean / hidden)[:, None])).astype(
        jnp.bfloat16
    )
    grad_passages = (p_inverse * (p_inner - p_normed * (p_mean / hidden)[:, None])).astype(
        jnp.bfloat16
    )
    gain_part = jnp.sum(grad_q * q_normed, axis=0) + jnp.sum(grad_p * p_normed, axis=0)
    gain_full = lax.dynamic_update_slice_in_dim(
        jnp.zeros((hidden,), jnp.float32), gain_part, member * piece, 0
    )
    loss_total, gain_total = lax.psum((loss_part, gain_full), ("dp", "group"))
    count = rows * n_data
    return (grad_queries, grad_passages, gain_total / math.sqrt(count), loss_total / count)


def solution(mesh):
    return jax.shard_map(
        local,
        mesh=mesh,
        in_specs=(P("dp", "group"), P("dp", "group"), P("dp", None), P("dp", None), P()),
        out_specs=(P("dp", "group"), P("dp", "group"), P(), P()),
        check_vma=False,
    )
```

```python
import functools
import math

import jax
import jax.numpy as jnp
from jax import lax
from jax.experimental import pallas as pl
from jax.experimental.pallas import tpu as pltpu
from jax.sharding import PartitionSpec as P

EPSILON = 1e-06
SOFTNESS_DIVISOR = 0.25
ROWS_BY_ROWS = (((1,), (1,)), ((), ()))
COLS_BY_COLS = (((0,), (0,)), ((), ()))
VMEM_BYTES = 56 << 20


def column(table, index):
    lane = lax.broadcasted_iota(jnp.int32, table.shape, 1)
    return jnp.sum(jnp.where(lane == index, table, jnp.zeros_like(table)), axis=1, keepdims=True)


def near_kernel(q_ref, p_ref, wanted_ref, near_ref):
    step = pl.program_id(1)

    @pl.when(step == 0)
    def _():
        near_ref[...] = jnp.zeros_like(near_ref)

    products = lax.dot_general(
        q_ref[0], p_ref[0], ROWS_BY_ROWS, preferred_element_type=jnp.float32
    )
    wanted = column(wanted_ref[0], step)
    place = lax.broadcasted_iota(jnp.int32, products.shape, 1)
    picked = jnp.sum(jnp.where(place == wanted, products, 0.0), axis=1, keepdims=True)
    lane = lax.broadcasted_iota(jnp.int32, near_ref.shape[1:], 1)
    near_ref[0] += jnp.where(lane == step, picked, 0.0)


def add_q_term(p_ref, wanted_ref, hard_ref, total_ref, step):
    wanted = column(wanted_ref[...], step)
    hard = column(hard_ref[...], step)
    rows = wanted.shape[0]
    place = lax.broadcasted_iota(jnp.int32, (rows, rows), 1)
    spread = jnp.where(place == wanted, hard, 0.0).astype(jnp.bfloat16)
    total_ref[...] += jnp.dot(spread, p_ref[0], preferred_element_type=jnp.float32)


def add_p_term(scale, q_ref, asked_ref, hard_ref, total_ref, step):
    hard = column(hard_ref[...], step) * scale
    pairs = (hard * q_ref[0].astype(jnp.float32)).astype(jnp.bfloat16)
    rows = pairs.shape[0]
    row = lax.broadcasted_iota(jnp.int32, (rows, rows), 0)
    select = jnp.where(row == asked_ref[0], 1.0, 0.0).astype(jnp.bfloat16)
    total_ref[...] += jnp.dot(select, pairs, preferred_element_type=jnp.float32)


def own_q_kernel(weights_ref, own_ref, p_ref, wanted_ref, hard_ref, grad_ref):
    step = pl.program_id(0)

    @pl.when(step == 0)
    def _():
        grad_ref[...] = jnp.dot(
            weights_ref[...], own_ref[...], preferred_element_type=jnp.float32
        )

    add_q_term(p_ref, wanted_ref, hard_ref, grad_ref, step)


def own_p_kernel(scale, weights_ref, own_ref, q_ref, asked_ref, hard_ref, grad_ref):
    step = pl.program_id(0)

    @pl.when(step == 0)
    def _():
        grad_ref[...] = scale * lax.dot_general(
            weights_ref[...], own_ref[...], COLS_BY_COLS, preferred_element_type=jnp.float32
        )

    add_p_term(scale, q_ref, asked_ref, hard_ref, grad_ref, step)


def sent_q_kernel(p_ref, wanted_ref, hard_ref, grad_ref, total_ref):
    step = pl.program_id(0)

    @pl.when(step == 0)
    def _():
        total_ref[...] = jnp.zeros_like(total_ref)

    add_q_term(p_ref, wanted_ref, hard_ref, total_ref, step)

    @pl.when(step == pl.num_programs(0) - 1)
    def _():
        grad_ref[...] = total_ref[...].astype(grad_ref.dtype)


def sent_p_kernel(scale, q_ref, asked_ref, hard_ref, grad_ref, total_ref):
    step = pl.program_id(0)

    @pl.when(step == 0)
    def _():
        total_ref[...] = jnp.zeros_like(total_ref)

    add_p_term(scale, q_ref, asked_ref, hard_ref, total_ref, step)

    @pl.when(step == pl.num_programs(0) - 1)
    def _():
        grad_ref[...] = total_ref[...].astype(grad_ref.dtype)


def whole(shape):
    return pl.BlockSpec(shape, lambda step: (0,) * len(shape))


def block(shape):
    return pl.BlockSpec((1,) + shape, lambda step: (step, 0, 0))


def params():
    return pltpu.CompilerParams(vmem_limit_bytes=VMEM_BYTES)


def cost(blocks, rows, piece):
    return pl.CostEstimate(
        flops=2 * blocks * rows * rows * piece,
        bytes_accessed=2 * blocks * rows * piece,
        transcendentals=0,
    )


def call(kernel, blocks, in_specs, dtype, rows, piece):
    scratch = [] if dtype == jnp.float32 else [pltpu.VMEM((rows, piece), jnp.float32)]
    return pl.pallas_call(
        kernel,
        grid=(blocks,),
        in_specs=in_specs,
        out_specs=whole((rows, piece)),
        out_shape=jax.ShapeDtypeStruct((rows, piece), dtype),
        scratch_shapes=scratch,
        compiler_params=params(),
        cost_estimate=cost(blocks, rows, piece),
    )


def local(queries, passages, neg_owner, neg_row, gain):
    rows, piece = queries.shape
    n_data = lax.axis_size("dp")
    n_members = lax.axis_size("group")
    member = lax.axis_index("group")
    hidden = piece * n_members
    scale = 1.0 / (SOFTNESS_DIVISOR * math.sqrt(hidden))
    my_gain = lax.dynamic_slice_in_dim(gain, member * piece, piece, 0)
    q_values = queries.astype(jnp.float32)
    p_values = passages.astype(jnp.float32)
    q_square, p_square = lax.psum(
        (jnp.sum(q_values * q_values, axis=1), jnp.sum(p_values * p_values, axis=1)), "group"
    )
    q_inverse = lax.rsqrt(q_square / hidden + EPSILON)[:, None]
    p_inverse = lax.rsqrt(p_square / hidden + EPSILON)[:, None]
    q_emb = (q_values * q_inverse * my_gain).astype(jnp.bfloat16)
    p_emb = (p_values * p_inverse * my_gain).astype(jnp.bfloat16)

    lines = 2 ** (int(math.log2(n_data)) // 2)
    plane = n_data // lines
    line_groups = [[a * plane + b for a in range(lines)] for b in range(plane)]
    plane_groups = [[a * plane + b for b in range(plane)] for a in range(lines)]
    here = lax.rem(lax.axis_index("dp"), plane)

    def exchange(table, groups):
        flat = table.reshape(table.shape[0], -1)
        came = lax.all_to_all(
            flat, "dp", split_axis=0, concat_axis=0, axis_index_groups=groups, tiled=True
        )
        return came.reshape(table.shape)

    def partner_of(shift):
        return [
            (a * plane + b, a * plane + (b ^ shift)) for a in range(lines) for b in range(plane)
        ]

    def plane_order(table):
        parts = [lax.dynamic_index_in_dim(table, here ^ k, 1) for k in range(plane)]
        return jnp.concatenate(parts, axis=1)

    line_q = lax.all_gather(q_emb, "dp", axis_index_groups=line_groups)
    plane_p = jnp.stack(
        [p_emb] + [lax.ppermute(p_emb, "dp", partner_of(shift)) for shift in range(1, plane)]
    )
    p_later, _ = lax.optimization_barrier((p_emb, line_q))
    line_p = lax.all_gather(p_later, "dp", axis_index_groups=line_groups)

    owners = jnp.arange(n_data, dtype=jnp.int32)[:, None, None]
    named = neg_owner.T[None] == owners
    wanted = (jnp.sum(jnp.where(named, neg_row.T[None] + 1, 0), axis=1) - 1).reshape(
        lines, plane, rows
    )
    line_wanted = exchange(wanted, line_groups)
    plane_wanted = exchange(wanted.transpose(1, 0, 2), plane_groups).transpose(0, 2, 1)

    q_then, line_wanted, plane_wanted = lax.optimization_barrier(
        (q_emb, line_wanted, plane_wanted)
    )
    partial_scores = jnp.dot(q_then, p_emb.T, preferred_element_type=jnp.float32) * scale
    scores = lax.psum(partial_scores, "group")
    near_part = pl.pallas_call(
        near_kernel,
        grid=(lines, plane),
        in_specs=[
            pl.BlockSpec((1, rows, piece), lambda a, b: (a, 0, 0)),
            pl.BlockSpec((1, rows, piece), lambda a, b: (b, 0, 0)),
            pl.BlockSpec((1, rows, plane), lambda a, b: (a, 0, 0)),
        ],
        out_specs=pl.BlockSpec((1, rows, plane), lambda a, b: (a, 0, 0)),
        out_shape=jax.ShapeDtypeStruct((lines, rows, plane), jnp.float32),
        compiler_params=params(),
        cost_estimate=cost(n_data, rows, piece),
    )(line_q, plane_p, plane_order(line_wanted).transpose(0, 2, 1))
    line_near = plane_order(lax.psum(near_part.transpose(0, 2, 1) * scale, "group"))
    near = jnp.where(wanted >= 0, exchange(line_near, line_groups), -jnp.inf)
    near = near.reshape(n_data, rows)

    positive = (
        jnp.arange(rows, dtype=jnp.int32)[None, :] == jnp.arange(rows, dtype=jnp.int32)[:, None]
    )
    top = jnp.maximum(jnp.max(scores, axis=1), jnp.max(near, axis=0))
    total = jnp.sum(jnp.exp(scores - top[:, None]), axis=1) + jnp.sum(
        jnp.exp(near - top[None, :]), axis=0
    )
    lse = top + jnp.log(total)
    losses = lse - jnp.sum(jnp.where(positive, scores, 0.0), axis=1)
    weights = (jnp.exp(scores - lse[:, None]) - positive.astype(jnp.float32)).astype(jnp.bfloat16)
    hard = jnp.exp(near - lse[None, :]).astype(jnp.bfloat16).astype(jnp.float32)
    hard = hard.reshape(lines, plane, rows)

    share = rows // n_members
    loss_part = jnp.sum(lax.dynamic_slice_in_dim(losses, member * share, share, 0))

    line_hard = exchange(hard, line_groups)
    plane_hard = exchange(hard.transpose(1, 0, 2), plane_groups).transpose(0, 2, 1)

    def p_tables(target):
        asked = lax.dynamic_index_in_dim(line_wanted, target, 1, keepdims=True)
        asked_hard = lax.dynamic_index_in_dim(line_hard, target, 1, keepdims=False).T
        return asked, asked_hard

    def q_tables(target):
        return (
            lax.dynamic_index_in_dim(plane_wanted, target, 0, keepdims=False),
            lax.dynamic_index_in_dim(plane_hard, target, 0, keepdims=False),
        )

    p_specs = [block((rows, piece)), block((1, rows)), whole((rows, lines))]
    q_specs = [block((rows, piece)), whole((rows, lines)), whole((rows, lines))]
    batch_specs = [whole((rows, rows)), whole((rows, piece))]
    size = (rows, piece)
    shifts = range(plane - 1, 0, -1)

    p_parts = []
    for shift in shifts:
        part = call(
            functools.partial(sent_p_kernel, scale), lines, p_specs, jnp.bfloat16, *size
        )(line_q, *p_tables(here ^ shift))
        p_parts.append(lax.ppermute(part, "dp", partner_of(shift)))
    grad_p = call(
        functools.partial(own_p_kernel, scale), lines, batch_specs + p_specs, jnp.float32, *size
    )(weights, q_emb, line_q, *p_tables(here))
    q_parts = []
    for shift in shifts:
        part = call(sent_q_kernel, lines, q_specs, jnp.bfloat16, *size)(
            line_p, *q_tables(here ^ shift)
        )
        q_parts.append(lax.ppermute(part, "dp", partner_of(shift)))
    grad_q = call(own_q_kernel, lines, batch_specs + q_specs, jnp.float32, *size)(
        weights, p_emb, line_p, *q_tables(here)
    )
    for part in p_parts:
        grad_p = grad_p + part.astype(jnp.float32)
    for part in q_parts:
        grad_q = grad_q + part.astype(jnp.float32)
    grad_q = grad_q * scale

    q_normed = q_values * q_inverse
    p_normed = p_values * p_inverse
    q_inner = grad_q * my_gain
    p_inner = grad_p * my_gain
    q_mean, p_mean = lax.psum(
        (jnp.sum(q_inner * q_normed, axis=1), jnp.sum(p_inner * p_normed, axis=1)), "group"
    )
    grad_queries = (q_inverse * (q_inner - q_normed * (q_mean / hidden)[:, None])).astype(
        jnp.bfloat16
    )
    grad_passages = (p_inverse * (p_inner - p_normed * (p_mean / hidden)[:, None])).astype(
        jnp.bfloat16
    )
    gain_part = jnp.sum(grad_q * q_normed, axis=0) + jnp.sum(grad_p * p_normed, axis=0)
    chunk = piece // n_data
    loss_column = jnp.full((n_data, 1), loss_part)
    shares = jnp.concatenate([gain_part.reshape(n_data, chunk), loss_column], axis=1)
    summed = jnp.sum(lax.all_to_all(shares, "dp", 0, 0, tiled=True), axis=0)
    copies = jnp.broadcast_to(summed[None], (n_data * n_members, chunk + 1))
    everyone = lax.all_to_all(copies, ("dp", "group"), 0, 0, tiled=True)
    everyone = everyone.reshape(n_data, n_members, chunk + 1)
    gain_total = everyone[:, :, :chunk].transpose(1, 0, 2).reshape(hidden)
    loss_total = jnp.sum(everyone[0, :, chunk])
    count = rows * n_data
    return (grad_queries, grad_passages, gain_total / math.sqrt(count), loss_total / count)


def solution(mesh):
    return jax.shard_map(
        local,
        mesh=mesh,
        in_specs=(P("dp", "group"), P("dp", "group"), P("dp", None), P("dp", None), P()),
        out_specs=(P("dp", "group"), P("dp", "group"), P(), P()),
        check_vma=False,
    )
```
